32 devices in a mesh: row: 8 (over z, core), col: 4 (over y, x).
Axes of the slice: x: 2, y: 2, z: 4, core: 2. Of those that a mesh axis runs over, the one named last changes fastest.
Arguments:
- features: bfloat16 [4096, 128], P(('row', 'col')), may hold values from -6 to 6
- tiles: bfloat16 [8, 4, 32, 128, 128], P('row', 'col'), may hold values from -0.125 to 0.125
- tile_index: int32 [8, 4, 32], P('row', 'col'), may hold values from 0 to 31, as said below
- tile_count: int32 [8, 4], P('row', 'col'), may hold values from 4 to 32, as said below
- w_first: bfloat16 [128, 256], replicated, may hold values from -0.5 to 0.5
- b_first: float32 [256], replicated, may hold values from -3 to 3
- w_second: bfloat16 [256, 128], replicated, may hold values from -0.375 to 0.375
- b_second: float32 [128], replicated, may hold values from -3 to 3
Outputs:
- logits: float32 [4096, 128], P(('row', 'col'))
The draws below stay inside these ranges and needn't reach their ends.
Inputs may be any that keep to these rules, and one draw needn't show every extreme that they name: `tile_index`: within one device the live slots name distinct tiles. `tile_count`: some device has all 32 slots live; every count is 32 divided by 1, 2, 4 or 8.
All inputs are finite; a program needn't handle non-finite values.
Results may differ from the reference program's by a relative error of at most 0.01.
Values may be sent and summed in bfloat16 or wider, within the bound.
A program may use at most 64 MiB of HBM per device.

```python
import jax
import jax.numpy as jnp
from jax import lax

F_IN = 128
HID = 256
OUT = 128
TILE = 128
NODE_DEV = 128
RT = 4
CT = 8
MAXT = 32
NODES = 4096
N_ROW = 8
N_COL = 4


def draw_tile_index(key, part):
    keys = jax.random.split(key, N_ROW * N_COL)
    picked = jax.vmap(lambda one_key: jax.random.permutation(one_key, RT * CT)[:MAXT])(keys)
    return picked.reshape(N_ROW, N_COL, MAXT).astype(jnp.int32)


def draw_tile_count(key, part):
    halvings = jax.random.randint(key, (N_ROW * N_COL,), 0, 4)
    counts = jnp.right_shift(jnp.full((N_ROW * N_COL,), MAXT, jnp.int32), halvings.astype(jnp.int32))
    busiest = jax.random.randint(jax.random.fold_in(key, 7), (), 0, N_ROW * N_COL)
    counts = counts.at[busiest].set(MAXT)
    return counts.reshape(N_ROW, N_COL).astype(jnp.int32)


def levels(key, dims, cuts, low, top_value):
    def one(position, parts):
        heights = jax.random.uniform(jax.random.fold_in(jax.random.fold_in(key, 6), position), (parts,), jnp.float32, low / len(cuts), top_value / len(cuts))
        return jnp.repeat(jnp.exp(heights), dims[position] // parts).reshape((-1,) + (1,) * (len(dims) - position - 1))

    loudness = one(*cuts[0])
    for cut in cuts[1:]:
        loudness = loudness * one(*cut)
    return loudness


def gaussian(own_key, shape, spread, limit, shards=(), held_as=jnp.bfloat16):
    result = jax.random.normal(own_key, shape, jnp.float32) * spread
    if len(shards) > 0:
        result = levels(own_key, shape, shards, -0.22, 0.18) * result
    return jnp.clip(result, min=-limit, max=limit).astype(held_as)


def setup_inputs(seed: int = 0) -> dict:
    key_of = jax.random.split(jax.random.key(seed), 9)
    features = gaussian(key_of[0], (NODES, F_IN), 1.0, 6.0, ((0, 32),))
    tiles = gaussian(key_of[1], (N_ROW, N_COL, MAXT, TILE, TILE), (TILE * MAXT * N_COL // (2 * RT)) ** -0.5, 0.125, ((0, 8), (1, 4)))
    tile_index = draw_tile_index(jax.random.fold_in(key_of[8], 71), 0)
    tile_count = draw_tile_count(jax.random.fold_in(key_of[8], 71), 0)
    w_first = gaussian(key_of[4], (F_IN, HID), F_IN ** -0.5, 0.5)
    b_first = gaussian(key_of[5], (HID,), 0.5, 3.0, (), jnp.float32)
    w_second = gaussian(key_of[6], (HID, OUT), HID ** -0.5, 0.375)
    b_second = gaussian(key_of[7], (OUT,), 0.5, 3.0, (), jnp.float32)
    return {"features": features, "tiles": tiles, "tile_index": tile_index, "tile_count": tile_count, "w_first": w_first, "b_first": b_first, "w_second": w_second, "b_second": b_second}


def aggregate(tiles, tile_index, tile_count, node_feats):
    feat_width = node_feats.shape[1]
    col_blocks = node_feats.reshape(N_ROW, N_COL, NODE_DEV, feat_width).transpose(1, 0, 2, 3).reshape(N_COL, CT, TILE, feat_width)

    def one_device(packed):
        tile_block, slot_index, live_count, col_tiles = packed
        picked = jnp.take(col_tiles, slot_index % CT, axis=0).astype(jnp.float32)
        products = jnp.einsum("mab,mbf->maf", tile_block.astype(jnp.float32), picked)
        live_mask = jnp.arange(MAXT, dtype=jnp.int32) < live_count
        placing = (((slot_index // CT)[:, None] == jnp.arange(RT, dtype=jnp.int32)[None, :]) & live_mask[:, None]).astype(jnp.float32)
        return jnp.einsum("mr,maf->raf", placing, products).reshape(RT * TILE, feat_width)

    def one_row(packed):
        tile_row, index_row, count_row = packed
        partials = lax.map(one_device, (tile_row, index_row, count_row, col_blocks))
        return jnp.sum(partials, axis=0)

    row_sums = lax.map(one_row, (tiles, tile_index, tile_count))
    return row_sums.reshape(N_ROW * N_COL * NODE_DEV, feat_width)


def reference(features, tiles, tile_index, tile_count, w_first, b_first, w_second, b_second):
    agg_first = aggregate(tiles, tile_index, tile_count, features).astype(jnp.bfloat16)
    hidden = jnp.maximum(jnp.dot(agg_first, w_first, preferred_element_type=jnp.float32) + b_first, 0.0).astype(jnp.bfloat16)
    projected = jnp.dot(hidden, w_second, preferred_element_type=jnp.float32).astype(jnp.bfloat16)
    return aggregate(tiles, tile_index, tile_count, projected) + b_second
```

```python
import functools

import jax
import jax.numpy as jnp
from jax import lax
from jax.experimental import pallas as pl
from jax.experimental.pallas import tpu as pltpu
from jax.sharding import PartitionSpec as P

CORES = 2


def tile_sum(columns, tile_block, slot_index, live_count, node_rows):
    tile_size = tile_block.shape[-1]
    feat_width = columns.shape[1]
    col_tiles = columns.reshape(columns.shape[0] // tile_size, tile_size, feat_width)
    tile_cols = col_tiles.shape[0]
    row_tiles = lax.axis_size("col") * node_rows // tile_size
    picked = jnp.take(col_tiles, slot_index % tile_cols, axis=0)
    products = jnp.einsum("mab,mbf->maf", tile_block, picked, preferred_element_type=jnp.float32)
    live_mask = jnp.arange(slot_index.shape[0], dtype=jnp.int32) < live_count
    placing = (
        ((slot_index // tile_cols)[:, None] == jnp.arange(row_tiles, dtype=jnp.int32)[None, :])
        & live_mask[:, None]
    ).astype(jnp.float32)
    partial_value = jnp.einsum("mr,maf->raf", placing, products)
    return partial_value.reshape(row_tiles * tile_size, feat_width)


def aggregate(node_feats, tile_block, slot_index, live_count):
    node_rows = node_feats.shape[0]
    gathered = lax.all_gather(node_feats, "row", axis=0, tiled=True)
    partial_value = tile_sum(gathered, tile_block, slot_index, live_count, node_rows)
    return lax.psum_scatter(partial_value, "col", scatter_dimension=0, tiled=True)


def sparse_local(features, tiles, tile_index, tile_count, w_first, b_first, w_second, b_second):
    tile_block = tiles[0, 0]
    slot_index = tile_index[0, 0]
    live_count = tile_count[0, 0]
    first_agg = aggregate(features, tile_block, slot_index, live_count).astype(jnp.bfloat16)
    hidden = jnp.maximum(
        jnp.dot(first_agg, w_first, preferred_element_type=jnp.float32) + b_first, 0.0
    ).astype(jnp.bfloat16)
    projected = jnp.dot(hidden, w_second, preferred_element_type=jnp.float32).astype(jnp.bfloat16)
    second = aggregate(projected, tile_block, slot_index, live_count)
    return second + b_second


def kernel(
    n_row, n_col,
    feats, tiles, index, count, w1, b1, w2, b2, out,
    tiles_v, index_s, count_s, w1_v, b1_v, w2_v, b2_v, adj, x1, x2,
    part_out, part_in,
    local_sem, gather_send, gather_recv, sib_send, sib_recv, part_send, part_recv,
):
    node_rows = feats.shape[0]
    slots, tile = tiles.shape[2], tiles.shape[3]
    n_chip = n_row // CORES
    tile_cols = n_row * node_rows // tile
    row, col = lax.axis_index("row"), lax.axis_index("col")
    chip, core = lax.div(row, CORES), lax.rem(row, CORES)
    sibling = chip * CORES + (1 - core)

    def at_chip(step):
        return lax.rem(chip + step + n_chip, n_chip) * CORES + core

    def at_col(step):
        return lax.rem(col + step + n_col, n_col)

    def rows(block):
        return pl.ds(pl.multiple_of(block * node_rows, node_rows), node_rows)

    loads = [
        pltpu.make_async_copy(index, index_s, local_sem.at[0]),
        pltpu.make_async_copy(count, count_s, local_sem.at[1]),
        pltpu.make_async_copy(tiles.at[0, 0], tiles_v.at[pl.ds(0, slots)], local_sem.at[2]),
        pltpu.make_async_copy(feats, x1.at[rows(row)], local_sem.at[3]),
        pltpu.make_async_copy(w1, w1_v, local_sem.at[4]),
        pltpu.make_async_copy(b1, b1_v, local_sem.at[5]),
        pltpu.make_async_copy(w2, w2_v, local_sem.at[6]),
        pltpu.make_async_copy(b2, b2_v, local_sem.at[7]),
    ]

    barrier = pltpu.get_barrier_semaphore()
    greeted = [{"row": at_chip(k), "col": col} for k in range(1, n_chip)]
    greeted += [{"row": sibling, "col": col}]
    greeted += [{"row": row, "col": at_col(k)} for k in range(1, n_col)]
    for device in greeted:
        pl.semaphore_signal(barrier, inc=1, device_id=device, device_id_type=pl.DeviceIdType.MESH)
    for load in loads:
        load.start()
    pl.semaphore_wait(barrier, len(greeted))

    def remote(src, dst, send_sem, recv_sem, device):
        return pltpu.make_async_remote_copy(
            src_ref=src, dst_ref=dst, send_sem=send_sem, recv_sem=recv_sem,
            device_id=device, device_id_type=pl.DeviceIdType.MESH,
        )

    def gather_start(layer, src, x):
        sends = []
        for k in range(1, n_chip):
            sends.append(remote(
                src, x.at[rows(row)], gather_send.at[layer, k - 1], gather_recv.at[layer, k - 1],
                {"row": at_chip(k), "col": col},
            ))
        sends.append(remote(
            src, x.at[rows(row)], sib_send.at[layer, 0], sib_recv.at[layer, 0],
            {"row": sibling, "col": col},
        ))
        for send in sends:
            send.start()
        return sends

    def gather_finish(layer, x, sends):
        for k in range(1, n_chip):
            sends[k - 1].wait_recv()
            block = x.at[rows(at_chip(-k))]
            forward = remote(
                block, block, sib_send.at[layer, k], sib_recv.at[layer, k],
                {"row": sibling, "col": col},
            )
            forward.start()
            sends.append(forward)
        for send in sends[n_chip - 1:]:
            send.wait_recv()

    def reduce_scatter(layer, x):
        sends = []
        for k in range(1, n_col):
            target = at_col(k)
            part_out[layer, k - 1] = jnp.dot(
                adj[rows(target), :], x[...], preferred_element_type=jnp.float32
            ).astype(part_out.dtype)
            send = remote(
                part_out.at[layer, k - 1], part_in.at[layer, k - 1],
                part_send.at[layer, k - 1], part_recv.at[layer, k - 1],
                {"row": row, "col": target},
            )
            send.start()
            sends.append(send)
        total = jnp.dot(adj[rows(col), :], x[...], preferred_element_type=jnp.float32)
        for k in range(1, n_col):
            sends[k - 1].wait_recv()
            total = total + part_in[layer, k - 1].astype(jnp.float32)
        return total, sends

    first_sends = gather_start(0, feats, x1)

    tiles_v[slots] = jnp.zeros(tiles_v.shape[1:], tiles_v.dtype)
    for load in loads[:4]:
        load.wait()
    live = count_s[0, 0]

    def place(position, carry):
        found = jnp.int32(slots)
        for slot in range(slots):
            hit = (index_s[0, 0, slot] == position) & (slot < live)
            found = jnp.where(hit, jnp.int32(slot), found)
        r = lax.div(position, tile_cols)
        c = lax.rem(position, tile_cols)
        adj[
            pl.ds(pl.multiple_of(r * tile, tile), tile), pl.ds(pl.multiple_of(c * tile, tile), tile)
        ] = tiles_v[found]
        return carry

    lax.fori_loop(0, adj.shape[0] // tile * tile_cols, place, 0)

    gather_finish(0, x1, first_sends)
    total, first_parts = reduce_scatter(0, x1)
    for load in loads[4:]:
        load.wait()
    hidden = jnp.maximum(
        jnp.dot(total.astype(jnp.bfloat16), w1_v[...], preferred_element_type=jnp.float32)
        + b1_v[...].reshape(1, -1), 0.0
    ).astype(jnp.bfloat16)
    x2[rows(row), :] = jnp.dot(hidden, w2_v[...], preferred_element_type=jnp.float32).astype(jnp.bfloat16)

    second_sends = gather_start(1, x2.at[rows(row)], x2)
    gather_finish(1, x2, second_sends)
    total, second_parts = reduce_scatter(1, x2)
    out[...] = total + b2_v[...].reshape(1, -1)
    for send in first_sends + first_parts + second_sends + second_parts:
        send.wait_send()


def dense_local(n_row, n_col, features, tiles, tile_index, tile_count, w_first, b_first, w_second, b_second):
    node_rows, f_in = features.shape
    slots, tile = tiles.shape[2], tiles.shape[3]
    width = w_second.shape[1]
    n_chip = n_row // CORES
    dma = pltpu.SemaphoreType.DMA
    return pl.pallas_call(
        functools.partial(kernel, n_row, n_col),
        out_shape=jax.ShapeDtypeStruct((node_rows, width), jnp.float32),
        in_specs=[pl.BlockSpec(memory_space=pl.ANY)] * 8,
        out_specs=pl.BlockSpec(memory_space=pltpu.VMEM),
        scratch_shapes=[
            pltpu.VMEM((slots + 1, tile, tile), tiles.dtype),
            pltpu.SMEM(tile_index.shape, jnp.int32),
            pltpu.SMEM(tile_count.shape, jnp.int32),
            pltpu.VMEM(w_first.shape, w_first.dtype),
            pltpu.VMEM(b_first.shape, b_first.dtype),
            pltpu.VMEM(w_second.shape, w_second.dtype),
            pltpu.VMEM(b_second.shape, b_second.dtype),
            pltpu.VMEM((n_col * node_rows, n_row * node_rows), tiles.dtype),
            pltpu.VMEM((n_row * node_rows, f_in), jnp.bfloat16),
            pltpu.VMEM((n_row * node_rows, width), jnp.bfloat16),
            pltpu.VMEM((2, n_col - 1, node_rows, width), jnp.bfloat16),
            pltpu.VMEM((2, n_col - 1, node_rows, width), jnp.bfloat16),
            dma((8,)),
            dma((2, n_chip - 1)),
            dma((2, n_chip - 1)),
            dma((2, n_chip)),
            dma((2, n_chip)),
            dma((2, n_col - 1)),
            dma((2, n_col - 1)),
        ],
        compiler_params=pltpu.CompilerParams(
            collective_id=0, has_side_effects=True, vmem_limit_bytes=16 * 2**20
        ),
    )(features, tiles, tile_index, tile_count, w_first, b_first, w_second, b_second)


def solution(mesh):
    in_specs = (
        P(("row", "col"), None),
        P("row", "col", None, None, None),
        P("row", "col", None),
        P("row", "col"),
        P(),
        P(),
        P(),
        P(),
    )
    out_specs = P(("row", "col"), None)
    n_row, n_col = mesh.shape["row"], mesh.shape["col"]

    def local(features, tiles, *rest):
        node_rows, (slots, tile) = features.shape[0], tiles.shape[2:4]
        positions = (n_row * node_rows // tile) * (n_col * node_rows // tile)
        fits = (
            n_row % CORES == 0 and n_row > CORES and n_col > 1 and node_rows % tile == 0
            and features.shape[1] == rest[4].shape[1] and positions <= 2 * slots
        )
        if fits:
            return dense_local(n_row, n_col, features, tiles, *rest)
        return sparse_local(features, tiles, *rest)

    return jax.shard_map(local, mesh=mesh, in_specs=in_specs, out_specs=out_specs, check_vma=False)
```

```python
import functools

import jax
import jax.numpy as jnp
from jax import lax
from jax.experimental import pallas as pl
from jax.experimental.pallas import tpu as pltpu
from jax.sharding import PartitionSpec as P

CORES = 2


def tile_sum(columns, tile_block, slot_index, live_count, node_rows):
    tile_size = tile_block.shape[-1]
    feat_width = columns.shape[1]
    col_tiles = columns.reshape(columns.shape[0] // tile_size, tile_size, feat_width)
    tile_cols = col_tiles.shape[0]
    row_tiles = lax.axis_size("col") * node_rows // tile_size
    picked = jnp.take(col_tiles, slot_index % tile_cols, axis=0)
    products = jnp.einsum("mab,mbf->maf", tile_block, picked, preferred_element_type=jnp.float32)
    live_mask = jnp.arange(slot_index.shape[0], dtype=jnp.int32) < live_count
    placing = (
        ((slot_index // tile_cols)[:, None] == jnp.arange(row_tiles, dtype=jnp.int32)[None, :])
        & live_mask[:, None]
    ).astype(jnp.float32)
    partial_value = jnp.einsum("mr,maf->raf", placing, products)
    return partial_value.reshape(row_tiles * tile_size, feat_width)


def aggregate(node_feats, tile_block, slot_index, live_count):
    node_rows = node_feats.shape[0]
    gathered = lax.all_gather(node_feats, "row", axis=0, tiled=True)
    partial_value = tile_sum(gathered, tile_block, slot_index, live_count, node_rows)
    return lax.psum_scatter(partial_value, "col", scatter_dimension=0, tiled=True)


def sparse_local(features, tiles, tile_index, tile_count, w_first, b_first, w_second, b_second):
    tile_block = tiles[0, 0]
    slot_index = tile_index[0, 0]
    live_count = tile_count[0, 0]
    first_agg = aggregate(features, tile_block, slot_index, live_count).astype(jnp.bfloat16)
    hidden = jnp.maximum(
        jnp.dot(first_agg, w_first, preferred_element_type=jnp.float32) + b_first, 0.0
    ).astype(jnp.bfloat16)
    projected = jnp.dot(hidden, w_second, preferred_element_type=jnp.float32).astype(jnp.bfloat16)
    second = aggregate(projected, tile_block, slot_index, live_count)
    return second + b_second


def kernel(
    n_row, n_col,
    feats, tiles, index, count, w1, b1, w2, b2, out,
    tiles_v, index_v, count_s, w1_v, b1_v, w2_v, b2_v, adj, x1, x2,
    part_out, part_in,
    local_sem, gather_send, gather_recv, sib_send, sib_recv, part_send, part_recv,
):
    node_rows = feats.shape[0]
    slots, tile = tiles.shape[2], tiles.shape[3]
    n_chip = n_row // CORES
    tile_cols = n_row * node_rows // tile
    row, col = lax.axis_index("row"), lax.axis_index("col")
    chip, core = lax.div(row, CORES), lax.rem(row, CORES)
    sibling = chip * CORES + (1 - core)

    def at_chip(step):
        return lax.rem(chip + step + n_chip, n_chip) * CORES + core

    def at_col(step):
        return lax.rem(col + step + n_col, n_col)

    def rows(block):
        return pl.ds(pl.multiple_of(block * node_rows, node_rows), node_rows)

    loads = [
        pltpu.make_async_copy(index, index_v, local_sem.at[0]),
        pltpu.make_async_copy(count, count_s, local_sem.at[1]),
        pltpu.make_async_copy(tiles.at[0, 0], tiles_v.at[pl.ds(0, slots)], local_sem.at[2]),
        pltpu.make_async_copy(feats, x1.at[rows(row)], local_sem.at[3]),
        pltpu.make_async_copy(w1, w1_v, local_sem.at[4]),
        pltpu.make_async_copy(b1, b1_v, local_sem.at[5]),
        pltpu.make_async_copy(w2, w2_v, local_sem.at[6]),
        pltpu.make_async_copy(b2, b2_v, local_sem.at[7]),
    ]

    barrier = pltpu.get_barrier_semaphore()
    greeted = [{"row": at_chip(k), "col": col} for k in range(1, n_chip)]
    greeted += [{"row": sibling, "col": col}]
    greeted += [{"row": row, "col": at_col(k)} for k in range(1, n_col)]
    for device in greeted:
        pl.semaphore_signal(barrier, inc=1, device_id=device, device_id_type=pl.DeviceIdType.MESH)
    for load in loads:
        load.start()

    tiles_v[slots] = jnp.zeros(tiles_v.shape[1:], tiles_v.dtype)
    for load in loads[:2]:
        load.wait()
    n_pos = adj.shape[0] // tile * tile_cols
    slot = lax.broadcasted_iota(jnp.int32, (n_pos, slots), 1)
    position = lax.broadcasted_iota(jnp.int32, (n_pos, slots), 0)
    hit = (index_v[0] == position) & (slot < count_s[0, 0])
    slot_at = jnp.min(jnp.where(hit, slot, slots), axis=1, keepdims=True)

    pl.semaphore_wait(barrier, len(greeted))

    def remote(src, dst, send_sem, recv_sem, device):
        return pltpu.make_async_remote_copy(
            src_ref=src, dst_ref=dst, send_sem=send_sem, recv_sem=recv_sem,
            device_id=device, device_id_type=pl.DeviceIdType.MESH,
        )

    def gather_start(layer, src, x):
        sends = []
        for k in range(1, n_chip):
            sends.append(remote(
                src, x.at[rows(row)], gather_send.at[layer, k - 1], gather_recv.at[layer, k - 1],
                {"row": at_chip(k), "col": col},
            ))
        sends.append(remote(
            src, x.at[rows(row)], sib_send.at[layer, 0], sib_recv.at[layer, 0],
            {"row": sibling, "col": col},
        ))
        for send in sends:
            send.start()
        return sends

    def gather_finish(layer, x, sends):
        for k in range(1, n_chip):
            sends[k - 1].wait_recv()
            block = x.at[rows(at_chip(-k))]
            forward = remote(
                block, block, sib_send.at[layer, k], sib_recv.at[layer, k],
                {"row": sibling, "col": col},
            )
            forward.start()
            sends.append(forward)
        for send in sends[n_chip - 1:]:
            send.wait_recv()

    def reduce_scatter(layer, x):
        sends = []
        for k in range(1, n_col):
            target = at_col(k)
            part_out[layer, k - 1] = jnp.dot(
                adj[rows(target), :], x[...], preferred_element_type=jnp.float32
            ).astype(part_out.dtype)
            send = remote(
                part_out.at[layer, k - 1], part_in.at[layer, k - 1],
                part_send.at[layer, k - 1], part_recv.at[layer, k - 1],
                {"row": row, "col": target},
            )
            send.start()
            sends.append(send)
        total = jnp.dot(adj[rows(col), :], x[...], preferred_element_type=jnp.float32)
        for k in range(1, n_col):
            sends[k - 1].wait_recv()
            total = total + part_in[layer, k - 1].astype(jnp.float32)
        return total, sends

    first_sends = gather_start(0, feats, x1)

    for load in loads[2:4]:
        load.wait()
    for place in range(n_pos):
        r, c = place // tile_cols, place % tile_cols
        adj[r * tile:(r + 1) * tile, c * tile:(c + 1) * tile] = tiles_v[slot_at[place, 0]]

    gather_finish(0, x1, first_sends)
    total, first_parts = reduce_scatter(0, x1)
    for load in loads[4:]:
        load.wait()
    hidden = jnp.maximum(
        jnp.dot(total.astype(jnp.bfloat16), w1_v[...], preferred_element_type=jnp.float32)
        + b1_v[...].reshape(1, -1), 0.0
    ).astype(jnp.bfloat16)
    x2[rows(row), :] = jnp.dot(hidden, w2_v[...], preferred_element_type=jnp.float32).astype(jnp.bfloat16)

    second_sends = gather_start(1, x2.at[rows(row)], x2)
    gather_finish(1, x2, second_sends)
    total, second_parts = reduce_scatter(1, x2)
    out[...] = total + b2_v[...].reshape(1, -1)
    for send in first_sends + first_parts + second_sends + second_parts:
        send.wait_send()


def dense_local(n_row, n_col, features, tiles, tile_index, tile_count, w_first, b_first, w_second, b_second):
    node_rows, f_in = features.shape
    slots, tile = tiles.shape[2], tiles.shape[3]
    width = w_second.shape[1]
    n_chip = n_row // CORES
    dma = pltpu.SemaphoreType.DMA
    return pl.pallas_call(
        functools.partial(kernel, n_row, n_col),
        out_shape=jax.ShapeDtypeStruct((node_rows, width), jnp.float32),
        in_specs=[pl.BlockSpec(memory_space=pltpu.HBM)] * 8,
        out_specs=pl.BlockSpec(memory_space=pltpu.VMEM),
        scratch_shapes=[
            pltpu.VMEM((slots + 1, tile, tile), tiles.dtype),
            pltpu.VMEM(tile_index.shape, jnp.int32),
            pltpu.SMEM(tile_count.shape, jnp.int32),
            pltpu.VMEM(w_first.shape, w_first.dtype),
            pltpu.VMEM(b_first.shape, b_first.dtype),
            pltpu.VMEM(w_second.shape, w_second.dtype),
            pltpu.VMEM(b_second.shape, b_second.dtype),
            pltpu.VMEM((n_col * node_rows, n_row * node_rows), tiles.dtype),
            pltpu.VMEM((n_row * node_rows, f_in), jnp.bfloat16),
            pltpu.VMEM((n_row * node_rows, width), jnp.bfloat16),
            pltpu.VMEM((2, n_col - 1, node_rows, width), jnp.bfloat16),
            pltpu.VMEM((2, n_col - 1, node_rows, width), jnp.bfloat16),
            dma((8,)),
            dma((2, n_chip - 1)),
            dma((2, n_chip - 1)),
            dma((2, n_chip)),
            dma((2, n_chip)),
            dma((2, n_col - 1)),
            dma((2, n_col - 1)),
        ],
        compiler_params=pltpu.CompilerParams(
            collective_id=0, has_side_effects=True, vmem_limit_bytes=56 * 2**20
        ),
    )(features, tiles, tile_index, tile_count, w_first, b_first, w_second, b_second)


def solution(mesh):
    in_specs = (
        P(("row", "col"), None),
        P("row", "col", None, None, None),
        P("row", "col", None),
        P("row", "col"),
        P(),
        P(),
        P(),
        P(),
    )
    out_specs = P(("row", "col"), None)
    n_row, n_col = mesh.shape["row"], mesh.shape["col"]

    def local(features, tiles, *rest):
        node_rows, (slots, tile) = features.shape[0], tiles.shape[2:4]
        positions = (n_row * node_rows // tile) * (n_col * node_rows // tile)
        fits = (
            n_row % CORES == 0 and n_row > CORES and n_col > 1 and node_rows % tile == 0
            and features.shape[1] == rest[4].shape[1] and positions <= 2 * slots
        )
        if fits:
            return dense_local(n_row, n_col, features, tiles, *rest)
        return sparse_local(features, tiles, *rest)

    return jax.shard_map(local, mesh=mesh, in_specs=in_specs, out_specs=out_specs, check_vma=False)
```

```python
import functools

import jax
import jax.numpy as jnp
from jax import lax
from jax.experimental import pallas as pl
from jax.experimental.pallas import tpu as pltpu
from jax.sharding import PartitionSpec as P

CORES = 2


def tile_sum(columns, tile_block, slot_index, live_count, node_rows):
    tile_size = tile_block.shape[-1]
    feat_width = columns.shape[1]
    col_tiles = columns.reshape(columns.shape[0] // tile_size, tile_size, feat_width)
    tile_cols = col_tiles.shape[0]
    row_tiles = lax.axis_size("col") * node_rows // tile_size
    picked = jnp.take(col_tiles, slot_index % tile_cols, axis=0)
    products = jnp.einsum("mab,mbf->maf", tile_block, picked, preferred_element_type=jnp.float32)
    live_mask = jnp.arange(slot_index.shape[0], dtype=jnp.int32) < live_count
    placing = (
        ((slot_index // tile_cols)[:, None] == jnp.arange(row_tiles, dtype=jnp.int32)[None, :])
        & live_mask[:, None]
    ).astype(jnp.float32)
    partial_value = jnp.einsum("mr,maf->raf", placing, products)
    return partial_value.reshape(row_tiles * tile_size, feat_width)


def aggregate(node_feats, tile_block, slot_index, live_count):
    node_rows = node_feats.shape[0]
    gathered = lax.all_gather(node_feats, "row", axis=0, tiled=True)
    partial_value = tile_sum(gathered, tile_block, slot_index, live_count, node_rows)
    return lax.psum_scatter(partial_value, "col", scatter_dimension=0, tiled=True)


def sparse_local(features, tiles, tile_index, tile_count, w_first, b_first, w_second, b_second):
    tile_block = tiles[0, 0]
    slot_index = tile_index[0, 0]
    live_count = tile_count[0, 0]
    first_agg = aggregate(features, tile_block, slot_index, live_count).astype(jnp.bfloat16)
    hidden = jnp.maximum(
        jnp.dot(first_agg, w_first, preferred_element_type=jnp.float32) + b_first, 0.0
    ).astype(jnp.bfloat16)
    projected = jnp.dot(hidden, w_second, preferred_element_type=jnp.float32).astype(jnp.bfloat16)
    second = aggregate(projected, tile_block, slot_index, live_count)
    return second + b_second


def kernel(
    n_row, n_col,
    feats, tiles, index, count, w1, b1, w2, b2, out,
    tiles_v, index_v, count_s, w1_v, b1_v, w2_v, b2_v, adj, x1, x2,
    part_out, part_in,
    local_sem, gather_send, gather_recv, sib_send, sib_recv, part_send, part_recv,
):
    node_rows = feats.shape[0]
    slots, tile = tiles.shape[2], tiles.shape[3]
    n_chip = n_row // CORES
    tile_cols = n_row * node_rows // tile
    row, col = lax.axis_index("row"), lax.axis_index("col")
    chip, core = lax.div(row, CORES), lax.rem(row, CORES)
    sibling = chip * CORES + (1 - core)

    def at_chip(step):
        return lax.rem(chip + step + n_chip, n_chip) * CORES + core

    def at_col(step):
        return lax.rem(col + step + n_col, n_col)

    def rows(block):
        return pl.ds(pl.multiple_of(block * node_rows, node_rows), node_rows)

    loads = [
        pltpu.make_async_copy(index, index_v, local_sem.at[0]),
        pltpu.make_async_copy(count, count_s, local_sem.at[1]),
        pltpu.make_async_copy(tiles.at[0, 0], tiles_v.at[pl.ds(0, slots)], local_sem.at[2]),
        pltpu.make_async_copy(feats, x1.at[rows(row)], local_sem.at[3]),
        pltpu.make_async_copy(w1, w1_v, local_sem.at[4]),
        pltpu.make_async_copy(b1, b1_v, local_sem.at[5]),
        pltpu.make_async_copy(w2, w2_v, local_sem.at[6]),
        pltpu.make_async_copy(b2, b2_v, local_sem.at[7]),
    ]

    barrier = pltpu.get_barrier_semaphore()
    greeted = [{"row": at_chip(k), "col": col} for k in range(1, n_chip)]
    greeted += [{"row": sibling, "col": col}]
    greeted += [{"row": row, "col": at_col(k)} for k in range(1, n_col)]
    for device in greeted:
        pl.semaphore_signal(barrier, inc=1, device_id=device, device_id_type=pl.DeviceIdType.MESH)
    for load in loads:
        load.start()

    tiles_v[slots] = jnp.zeros(tiles_v.shape[1:], tiles_v.dtype)
    for load in loads[:2]:
        load.wait()
    n_pos = adj.shape[0] // tile * tile_cols
    slot = lax.broadcasted_iota(jnp.int32, (n_pos, slots), 1)
    position = lax.broadcasted_iota(jnp.int32, (n_pos, slots), 0)
    hit = (index_v[0] == position) & (slot < count_s[0, 0])
    slot_at = jnp.min(jnp.where(hit, slot, slots), axis=1, keepdims=True)

    pl.semaphore_wait(barrier, len(greeted))

    def remote(src, dst, send_sem, recv_sem, device):
        return pltpu.make_async_remote_copy(
            src_ref=src, dst_ref=dst, send_sem=send_sem, recv_sem=recv_sem,
            device_id=device, device_id_type=pl.DeviceIdType.MESH,
        )

    def gather_start(layer, src, x):
        sends = []
        for k in range(1, n_chip):
            sends.append(remote(
                src, x.at[rows(row)], gather_send.at[layer, k - 1], gather_recv.at[layer, k - 1],
                {"row": at_chip(k), "col": col},
            ))
        sends.append(remote(
            src, x.at[rows(row)], sib_send.at[layer, 0], sib_recv.at[layer, 0],
            {"row": sibling, "col": col},
        ))
        sends[-1].start()
        for k in range(1, n_chip):
            sends[k - 1].start()
        return sends

    def gather_finish(layer, x, sends):
        for k in range(1, n_chip):
            sends[k - 1].wait_recv()
            block = x.at[rows(at_chip(-k))]
            forward = remote(
                block, block, sib_send.at[layer, k], sib_recv.at[layer, k],
                {"row": sibling, "col": col},
            )
            forward.start()
            sends.append(forward)
        for send in sends[n_chip - 1:]:
            send.wait_recv()

    def reduce_scatter(layer, x):
        sends = []
        for k in range(1, n_col):
            target = at_col(k)
            part_out[layer, k - 1] = jnp.dot(
                adj[rows(target), :], x[...], preferred_element_type=jnp.float32
            ).astype(part_out.dtype)
            send = remote(
                part_out.at[layer, k - 1], part_in.at[layer, k - 1],
                part_send.at[layer, k - 1], part_recv.at[layer, k - 1],
                {"row": row, "col": target},
            )
            send.start()
            sends.append(send)
        total = jnp.dot(adj[rows(col), :], x[...], preferred_element_type=jnp.float32)
        for k in range(1, n_col):
            sends[k - 1].wait_recv()
            total = total + part_in[layer, k - 1].astype(jnp.float32)
        return total, sends

    loads[3].wait()
    first_sends = gather_start(0, x1.at[rows(row)], x1)

    loads[2].wait()
    for place in range(n_pos):
        r, c = place // tile_cols, place % tile_cols
        adj[r * tile:(r + 1) * tile, c * tile:(c + 1) * tile] = tiles_v[slot_at[place, 0]]

    gather_finish(0, x1, first_sends)
    total, first_parts = reduce_scatter(0, x1)
    for load in loads[4:]:
        load.wait()
    hidden = jnp.maximum(
        jnp.dot(total.astype(jnp.bfloat16), w1_v[...], preferred_element_type=jnp.float32)
        + b1_v[...].reshape(1, -1), 0.0
    ).astype(jnp.bfloat16)
    x2[rows(row), :] = jnp.dot(hidden, w2_v[...], preferred_element_type=jnp.float32).astype(jnp.bfloat16)

    second_sends = gather_start(1, x2.at[rows(row)], x2)
    gather_finish(1, x2, second_sends)
    total, second_parts = reduce_scatter(1, x2)
    out[...] = total + b2_v[...].reshape(1, -1)
    for send in first_sends + first_parts + second_sends + second_parts:
        send.wait_send()


def dense_local(n_row, n_col, features, tiles, tile_index, tile_count, w_first, b_first, w_second, b_second):
    node_rows, f_in = features.shape
    slots, tile = tiles.shape[2], tiles.shape[3]
    width = w_second.shape[1]
    n_chip = n_row // CORES
    dma = pltpu.SemaphoreType.DMA
    return pl.pallas_call(
        functools.partial(kernel, n_row, n_col),
        out_shape=jax.ShapeDtypeStruct((node_rows, width), jnp.float32),
        in_specs=[pl.BlockSpec(memory_space=pltpu.HBM)] * 8,
        out_specs=pl.BlockSpec(memory_space=pltpu.VMEM),
        scratch_shapes=[
            pltpu.VMEM((slots + 1, tile, tile), tiles.dtype),
            pltpu.VMEM(tile_index.shape, jnp.int32),
            pltpu.SMEM(tile_count.shape, jnp.int32),
            pltpu.VMEM(w_first.shape, w_first.dtype),
            pltpu.VMEM(b_first.shape, b_first.dtype),
            pltpu.VMEM(w_second.shape, w_second.dtype),
            pltpu.VMEM(b_second.shape, b_second.dtype),
            pltpu.VMEM((n_col * node_rows, n_row * node_rows), tiles.dtype),
            pltpu.VMEM((n_row * node_rows, f_in), jnp.bfloat16),
            pltpu.VMEM((n_row * node_rows, width), jnp.bfloat16),
            pltpu.VMEM((2, n_col - 1, node_rows, width), jnp.bfloat16),
            pltpu.VMEM((2, n_col - 1, node_rows, width), jnp.bfloat16),
            dma((8,)),
            dma((2, n_chip - 1)),
            dma((2, n_chip - 1)),
            dma((2, n_chip)),
            dma((2, n_chip)),
            dma((2, n_col - 1)),
            dma((2, n_col - 1)),
        ],
        compiler_params=pltpu.CompilerParams(
            collective_id=0, has_side_effects=True, vmem_limit_bytes=56 * 2**20
        ),
    )(features, tiles, tile_index, tile_count, w_first, b_first, w_second, b_second)


def solution(mesh):
    in_specs = (
        P(("row", "col"), None),
        P("row", "col", None, None, None),
        P("row", "col", None),
        P("row", "col"),
        P(),
        P(),
        P(),
        P(),
    )
    out_specs = P(("row", "col"), None)
    n_row, n_col = mesh.shape["row"], mesh.shape["col"]

    def local(features, tiles, *rest):
        node_rows, (slots, tile) = features.shape[0], tiles.shape[2:4]
        positions = (n_row * node_rows // tile) * (n_col * node_rows // tile)
        fits = (
            n_row % CORES == 0 and n_row > CORES and n_col > 1 and node_rows % tile == 0
            and features.shape[1] == rest[4].shape[1] and positions <= 2 * slots
        )
        if fits:
            return dense_local(n_row, n_col, features, tiles, *rest)
        return sparse_local(features, tiles, *rest)

    return jax.shard_map(local, mesh=mesh, in_specs=in_specs, out_specs=out_specs, check_vma=False)
```

```python
import functools

import jax
import jax.numpy as jnp
from jax import lax
from jax.experimental import pallas as pl
from jax.experimental.pallas import tpu as pltpu
from jax.sharding import PartitionSpec as P

CORES = 2


def tile_sum(columns, tile_block, slot_index, live_count, node_rows):
    tile_size = tile_block.shape[-1]
    feat_width = columns.shape[1]
    col_tiles = columns.reshape(columns.shape[0] // tile_size, tile_size, feat_width)
    tile_cols = col_tiles.shape[0]
    row_tiles = lax.axis_size("col") * node_rows // tile_size
    picked = jnp.take(col_tiles, slot_index % tile_cols, axis=0)
    products = jnp.einsum("mab,mbf->maf", tile_block, picked, preferred_element_type=jnp.float32)
    live_mask = jnp.arange(slot_index.shape[0], dtype=jnp.int32) < live_count
    placing = (
        ((slot_index // tile_cols)[:, None] == jnp.arange(row_tiles, dtype=jnp.int32)[None, :])
        & live_mask[:, None]
    ).astype(jnp.float32)
    partial_value = jnp.einsum("mr,maf->raf", placing, products)
    return partial_value.reshape(row_tiles * tile_size, feat_width)


def aggregate(node_feats, tile_block, slot_index, live_count):
    node_rows = node_feats.shape[0]
    gathered = lax.all_gather(node_feats, "row", axis=0, tiled=True)
    partial_value = tile_sum(gathered, tile_block, slot_index, live_count, node_rows)
    return lax.psum_scatter(partial_value, "col", scatter_dimension=0, tiled=True)


def sparse_local(features, tiles, tile_index, tile_count, w_first, b_first, w_second, b_second):
    tile_block = tiles[0, 0]
    slot_index = tile_index[0, 0]
    live_count = tile_count[0, 0]
    first_agg = aggregate(features, tile_block, slot_index, live_count).astype(jnp.bfloat16)
    hidden = jnp.maximum(
        jnp.dot(first_agg, w_first, preferred_element_type=jnp.float32) + b_first, 0.0
    ).astype(jnp.bfloat16)
    projected = jnp.dot(hidden, w_second, preferred_element_type=jnp.float32).astype(jnp.bfloat16)
    second = aggregate(projected, tile_block, slot_index, live_count)
    return second + b_second


def kernel(
    n_row, n_col,
    feats, tiles, index, count, w1, b1, w2, b2, out,
    tiles_v, index_v, count_s, w1_v, b1_v, w2_v, b2_v, adj, x1, x2,
    part_out, part_in,
    local_sem, gather_send, gather_recv, sib_send, sib_recv, part_send, part_recv,
):
    node_rows = feats.shape[0]
    slots, tile = tiles.shape[2], tiles.shape[3]
    n_chip = n_row // CORES
    tile_cols = n_row * node_rows // tile
    row, col = lax.axis_index("row"), lax.axis_index("col")
    chip, core = lax.div(row, CORES), lax.rem(row, CORES)
    sibling = chip * CORES + (1 - core)

    def at_chip(step):
        return lax.rem(chip + step + n_chip, n_chip) * CORES + core

    def at_col(step):
        return lax.rem(col + step + n_col, n_col)

    def rows(block):
        return pl.ds(pl.multiple_of(block * node_rows, node_rows), node_rows)

    loads = [
        pltpu.make_async_copy(index, index_v, local_sem.at[0]),
        pltpu.make_async_copy(count, count_s, local_sem.at[1]),
        pltpu.make_async_copy(tiles.at[0, 0], tiles_v.at[pl.ds(0, slots)], local_sem.at[2]),
        pltpu.make_async_copy(feats, x1.at[rows(row)], local_sem.at[3]),
        pltpu.make_async_copy(w1, w1_v, local_sem.at[4]),
        pltpu.make_async_copy(b1, b1_v, local_sem.at[5]),
        pltpu.make_async_copy(w2, w2_v, local_sem.at[6]),
        pltpu.make_async_copy(b2, b2_v, local_sem.at[7]),
    ]

    barrier = pltpu.get_barrier_semaphore()
    greeted = [{"row": at_chip(k), "col": col} for k in range(1, n_chip)]
    greeted += [{"row": sibling, "col": col}]
    greeted += [{"row": row, "col": at_col(k)} for k in range(1, n_col)]
    for device in greeted:
        pl.semaphore_signal(barrier, inc=1, device_id=device, device_id_type=pl.DeviceIdType.MESH)
    for load in loads:
        load.start()

    tiles_v[slots] = jnp.zeros(tiles_v.shape[1:], tiles_v.dtype)
    for load in loads[:2]:
        load.wait()
    n_pos = adj.shape[0] // tile * tile_cols
    slot = lax.broadcasted_iota(jnp.int32, (n_pos, slots), 1)
    position = lax.broadcasted_iota(jnp.int32, (n_pos, slots), 0)
    hit = (index_v[0] == position) & (slot < count_s[0, 0])
    slot_at = jnp.min(jnp.where(hit, slot, slots), axis=1, keepdims=True)

    pl.semaphore_wait(barrier, len(greeted))

    def remote(src, dst, send_sem, recv_sem, device):
        return pltpu.make_async_remote_copy(
            src_ref=src, dst_ref=dst, send_sem=send_sem, recv_sem=recv_sem,
            device_id=device, device_id_type=pl.DeviceIdType.MESH,
        )

    def gather_start(layer, src, x):
        sends = []
        for k in range(1, n_chip):
            sends.append(remote(
                src, x.at[rows(row)], gather_send.at[layer, k - 1], gather_recv.at[layer, k - 1],
                {"row": at_chip(k), "col": col},
            ))
        sends.append(remote(
            src, x.at[rows(row)], sib_send.at[layer, 0], sib_recv.at[layer, 0],
            {"row": sibling, "col": col},
        ))
        sends[-1].start()
        for k in range(1, n_chip):
            sends[k - 1].start()
        return sends

    def gather_finish(layer, x, sends):
        for k in range(1, n_chip):
            sends[k - 1].wait_recv()
            block = x.at[rows(at_chip(-k))]
            forward = remote(
                block, block, sib_send.at[layer, k], sib_recv.at[layer, k],
                {"row": sibling, "col": col},
            )
            forward.start()
            sends.append(forward)
        for send in sends[n_chip - 1:]:
            send.wait_recv()

    def reduce_scatter(layer, x):
        sends = {}
        for k in sorted(range(1, n_col), key=lambda k: -abs(2 * k - n_col)):
            target = at_col(k)
            part_out[layer, k - 1] = jnp.dot(
                adj[rows(target), :], x[...], preferred_element_type=jnp.float32
            ).astype(part_out.dtype)
            send = remote(
                part_out.at[layer, k - 1], part_in.at[layer, k - 1],
                part_send.at[layer, k - 1], part_recv.at[layer, k - 1],
                {"row": row, "col": target},
            )
            send.start()
            sends[k] = send
        total = jnp.dot(adj[rows(col), :], x[...], preferred_element_type=jnp.float32)
        for k in sends:
            sends[k].wait_recv()
            total = total + part_in[layer, k - 1].astype(jnp.float32)
        return total, list(sends.values())

    loads[3].wait()
    first_sends = gather_start(0, x1.at[rows(row)], x1)

    loads[2].wait()
    for place in range(n_pos):
        r, c = place // tile_cols, place % tile_cols
        adj[r * tile:(r + 1) * tile, c * tile:(c + 1) * tile] = tiles_v[slot_at[place, 0]]

    gather_finish(0, x1, first_sends)
    total, first_parts = reduce_scatter(0, x1)
    for load in loads[4:]:
        load.wait()
    hidden = jnp.maximum(
        jnp.dot(total.astype(jnp.bfloat16), w1_v[...], preferred_element_type=jnp.float32)
        + b1_v[...].reshape(1, -1), 0.0
    ).astype(jnp.bfloat16)
    x2[rows(row), :] = jnp.dot(hidden, w2_v[...], preferred_element_type=jnp.float32).astype(jnp.bfloat16)

    second_sends = gather_start(1, x2.at[rows(row)], x2)
    gather_finish(1, x2, second_sends)
    total, second_parts = reduce_scatter(1, x2)
    out[...] = total + b2_v[...].reshape(1, -1)
    for send in first_sends + first_parts + second_sends + second_parts:
        send.wait_send()


def dense_local(n_row, n_col, features, tiles, tile_index, tile_count, w_first, b_first, w_second, b_second):
    node_rows, f_in = features.shape
    slots, tile = tiles.shape[2], tiles.shape[3]
    width = w_second.shape[1]
    n_chip = n_row // CORES
    dma = pltpu.SemaphoreType.DMA
    return pl.pallas_call(
        functools.partial(kernel, n_row, n_col),
        out_shape=jax.ShapeDtypeStruct((node_rows, width), jnp.float32),
        in_specs=[pl.BlockSpec(memory_space=pltpu.HBM)] * 8,
        out_specs=pl.BlockSpec(memory_space=pltpu.VMEM),
        scratch_shapes=[
            pltpu.VMEM((slots + 1, tile, tile), tiles.dtype),
            pltpu.VMEM(tile_index.shape, jnp.int32),
            pltpu.SMEM(tile_count.shape, jnp.int32),
            pltpu.VMEM(w_first.shape, w_first.dtype),
            pltpu.VMEM(b_first.shape, b_first.dtype),
            pltpu.VMEM(w_second.shape, w_second.dtype),
            pltpu.VMEM(b_second.shape, b_second.dtype),
            pltpu.VMEM((n_col * node_rows, n_row * node_rows), tiles.dtype),
            pltpu.VMEM((n_row * node_rows, f_in), jnp.bfloat16),
            pltpu.VMEM((n_row * node_rows, width), jnp.bfloat16),
            pltpu.VMEM((2, n_col - 1, node_rows, width), jnp.bfloat16),
            pltpu.VMEM((2, n_col - 1, node_rows, width), jnp.bfloat16),
            dma((8,)),
            dma((2, n_chip - 1)),
            dma((2, n_chip - 1)),
            dma((2, n_chip)),
            dma((2, n_chip)),
            dma((2, n_col - 1)),
            dma((2, n_col - 1)),
        ],
        compiler_params=pltpu.CompilerParams(
            collective_id=0, has_side_effects=True, vmem_limit_bytes=56 * 2**20
        ),
    )(features, tiles, tile_index, tile_count, w_first, b_first, w_second, b_second)


def solution(mesh):
    in_specs = (
        P(("row", "col"), None),
        P("row", "col", None, None, None),
        P("row", "col", None),
        P("row", "col"),
        P(),
        P(),
        P(),
        P(),
    )
    out_specs = P(("row", "col"), None)
    n_row, n_col = mesh.shape["row"], mesh.shape["col"]

    def local(features, tiles, *rest):
        node_rows, (slots, tile) = features.shape[0], tiles.shape[2:4]
        positions = (n_row * node_rows // tile) * (n_col * node_rows // tile)
        fits = (
            n_row % CORES == 0 and n_row > CORES and n_col > 1 and node_rows % tile == 0
            and features.shape[1] == rest[4].shape[1] and positions <= 2 * slots
        )
        if fits:
            return dense_local(n_row, n_col, features, tiles, *rest)
        return sparse_local(features, tiles, *rest)

    return jax.shard_map(local, mesh=mesh, in_specs=in_specs, out_specs=out_specs, check_vma=False)
```
